128 devices in a mesh: req: 16 (over z, y), head: 8 (over x, core).
Axes of the slice: x: 4, y: 4, z: 4, core: 2. Of those that a mesh axis runs over, the one named last changes fastest.
Arguments:
- queries: bfloat16 [256, 64, 8192], P('req', None, 'head'), may hold values from -6 to 6
- keys: bfloat16 [256, 64, 8192], P('req', None, 'head'), may hold values from -1.5 to 1.5
- values: bfloat16 [256, 64, 8192], P('req', None, 'head'), may hold values from -6 to 6
- states: float32 [256, 64, 128, 128], P('req', 'head'), may hold values from -3 to 3
- parents: int32 [256, 64], P('req'), may hold values from -1 to 62, as said below
- path_nodes: int32 [256, 64], P('req'), may hold values from -1 to 63, as said below
- held: int32 [256], replicated, may hold values from 0 to 255, as said below
- rates: float32 [64], P('head'), may hold values from 0.004 to 0.15
- gain: float32 [8192], P('head'), may hold values from 0.5 to 2
Outputs:
- mixed: bfloat16 [256, 64, 8192], P('req', None, 'head')
- new_states: float32 [256, 64, 128, 128], P('req', 'head')
The draws below stay inside these ranges and needn't reach their ends.
Inputs may be any that keep to these rules, and one draw needn't show every extreme that they name: `parents`: node 0 has parent -1; every other node's parent is a lower-numbered node. `path_nodes`: a row lists the accepted path from node 0 down the tree, each entry a child of the one before, then -1 to the end. `held`: a permutation of the requests; each aligned block of 16 rows holds exactly 1 request of every aligned block of 16 requests.
All inputs are finite; a program needn't handle non-finite values.
Results may differ from the reference program's by a relative error of at most 0.0056.
Values may be sent and summed in bfloat16 or wider, within the bound.
No kernel may reach another device: no remote copies, remote signals or barrier semaphores. Data moves between devices by JAX's collectives and lax.ppermute only.
A program may use at most 128 MiB of HBM per device.

```python
import math
import jax
import jax.numpy as jnp
from jax import lax

HEADS = 64
HD = 128
NODES = 64
R_DEV = 16
REQS = 256


def tree_parts(key):
    key = jax.random.fold_in(key, 7)
    first, second, third = jax.random.split(key, 3)
    spread = jax.random.randint(first, (REQS, 1), 1, 9)
    hops = jax.random.randint(second, (REQS, NODES), 0, 1 << 20) % spread + 1
    column = jnp.arange(NODES, dtype=jnp.int32)
    parents = jnp.where(column[None, :] == 0, -1, jnp.maximum(column[None, :] - hops, 0)).astype(jnp.int32)
    walker = jax.random.randint(third, (REQS,), 0, NODES).astype(jnp.int32)
    trail = []
    for repeat in range(NODES):
        trail.append(walker)
        upward = jnp.take_along_axis(parents, jnp.maximum(walker, 0)[:, None], axis=1)[:, 0]
        walker = jnp.where(walker >= 0, upward, -1)
    trail = jnp.stack(trail, axis=1)
    length = jnp.sum((trail >= 0).astype(jnp.int32), axis=1)
    target = length[:, None] - 1 - column[None, :]
    path = jnp.where(target >= 0, jnp.take_along_axis(trail, jnp.maximum(target, 0), axis=1), -1)
    return (parents, path.astype(jnp.int32))


def draw_parents(key, part):
    return tree_parts(key)[0]


def draw_path_nodes(key, part):
    return tree_parts(key)[1]


def shuffled(subkey):
    return jax.random.permutation(subkey, R_DEV)


def draw_held(key, part):
    key = jax.random.fold_in(key, 13)
    first, second = jax.random.split(key)
    blocks = REQS // R_DEV
    dealt = jax.vmap(shuffled)(jax.random.split(first, blocks))
    idents = dealt + (jnp.arange(blocks, dtype=jnp.int32) * R_DEV)[:, None]
    idents = idents.reshape(blocks, blocks, R_DEV // blocks).transpose(1, 0, 2).reshape(blocks, R_DEV)
    mixing = jax.vmap(shuffled)(jax.random.split(second, blocks))
    idents = jnp.take_along_axis(idents, mixing, axis=1)
    return idents.reshape(REQS).astype(jnp.int32)


def steps_of(rng, shape, shards, low, high):
    def one(axis_at, shards_of):
        heights = jax.random.uniform(jax.random.fold_in(jax.random.fold_in(rng, 6), axis_at), (shards_of,), jnp.float32, low / len(shards), high / len(shards))
        return jnp.repeat(jnp.exp(heights), shape[axis_at] // shards_of).reshape((-1,) + (1,) * (len(shape) - axis_at - 1))

    factor_of = one(*shards[0])
    for cut in shards[1:]:
        factor_of = factor_of * one(*cut)
    return factor_of


def bell_draw(own_key, shape, scale, limit, shards=(), kind=jnp.bfloat16):
    values = scale * jax.random.normal(own_key, shape, jnp.float32)
    if shards:
        values = values * steps_of(own_key, shape, shards, -0.22, 0.18)
    return jnp.clip(values, -limit, limit).astype(kind)


def setup_inputs(seed: int = 0) -> dict:
    streams_of = jax.random.split(jax.random.key(seed), 10)
    queries = bell_draw(streams_of[0], (REQS, NODES, HEADS * HD), 1.0, 6.0, ((0, 16), (2, 8)))
    keys = bell_draw(streams_of[1], (REQS, NODES, HEADS * HD), 0.25, 1.5, ((0, 16), (2, 8)))
    values = bell_draw(streams_of[2], (REQS, NODES, HEADS * HD), 1.0, 6.0, ((0, 16), (2, 8)))
    states = bell_draw(streams_of[3], (REQS, HEADS, HD, HD), 0.5, 3.0, ((0, 16), (1, 8)), jnp.float32)
    parents = draw_parents(jax.random.fold_in(streams_of[9], 71), 0)
    path_nodes = draw_path_nodes(jax.random.fold_in(streams_of[9], 71), 0)
    held = draw_held(jax.random.fold_in(streams_of[9], 71), 0)
    rates = jnp.clip(jnp.exp(math.log(0.15) - 3.624341 * jax.random.uniform(streams_of[7], (HEADS,), jnp.float32) ** steps_of(streams_of[7], (HEADS,), ((0, 8),), -0.2, 0.2)), 0.004, 0.15)
    gain = jnp.clip(jnp.exp(math.log(2.0) - 1.3862944 * jax.random.uniform(streams_of[8], (HEADS * HD,), jnp.float32) ** steps_of(streams_of[8], (HEADS * HD,), ((0, 8),), -0.2, 0.2)), 0.5, 2.0)
    return {"queries": queries, "keys": keys, "values": values, "states": states, "parents": parents, "path_nodes": path_nodes, "held": held, "rates": rates, "gain": gain}


EPS = 1e-06
HIGH = lax.Precision.HIGHEST

def ancestry(parents):
    nodes = parents.shape[-1]
    column = jnp.arange(nodes, dtype=jnp.int32)
    step_map = (parents[:, :, None] == column[None, None, :]).astype(jnp.float32)
    reach = jnp.broadcast_to(jnp.eye(nodes, dtype=jnp.float32), step_map.shape)
    for repeat in range(nodes.bit_length()):
        reach = reach + jnp.einsum('rij,rjk->rik', step_map, reach, precision=HIGH)
        step_map = jnp.einsum('rij,rjk->rik', step_map, step_map, precision=HIGH)
    return reach

def attend(queries, keys, values, parents, path_nodes, states, rates):
    rows, nodes, width = queries.shape
    heads = rates.shape[0]
    size = width // heads
    q_heads = queries.reshape(rows, nodes, heads, size).astype(jnp.float32)
    k_heads = keys.reshape(rows, nodes, heads, size).astype(jnp.float32)
    v_heads = values.reshape(rows, nodes, heads, size).astype(jnp.float32)
    reach = ancestry(parents)
    depth = lax.optimization_barrier(jnp.sum(reach, axis=-1))
    column = jnp.arange(nodes, dtype=jnp.int32)
    onpath = lax.optimization_barrier(jnp.sum((path_nodes[:, :, None] == column[None, None, :]).astype(jnp.float32), axis=1))
    length = lax.optimization_barrier(jnp.sum((path_nodes >= 0).astype(jnp.float32), axis=1))
    spacing = jnp.maximum(depth[:, :, None] - depth[:, None, :], 0.0)
    fading = jnp.exp(-rates[None, :, None, None] * spacing[:, None]) * reach[:, None]
    scores = jnp.einsum('rnhd,rmhd->rhnm', q_heads, k_heads, precision=HIGH)
    weights = lax.optimization_barrier((scores * fading).astype(jnp.bfloat16)).astype(jnp.float32)
    local = jnp.einsum('rhnm,rmhd->rnhd', weights, v_heads, precision=HIGH)
    prior = jnp.einsum('rnhd,rhde->rnhe', q_heads, states, precision=HIGH)
    prior = prior * jnp.exp(-rates[None, None, :, None] * depth[:, :, None, None])
    attn = (local + prior).astype(jnp.bfloat16).reshape(rows, nodes, width)
    leading = jnp.exp(-rates[None, :] * length[:, None])
    path_weight = onpath[:, None, :] * jnp.exp(-rates[None, :, None] * (length[:, None, None] - depth[:, None, :]))
    scaled_keys = k_heads * jnp.transpose(path_weight, (0, 2, 1))[:, :, :, None]
    update = jnp.einsum('rnhd,rnhe->rhde', scaled_keys, v_heads, precision=HIGH)
    fresh = leading[:, :, None, None] * states + update
    return (attn, fresh)

def reference(queries, keys, values, states, parents, path_nodes, held, rates, gain):

    def one_row(item):
        index, state, parent, path = item
        attn, fresh = attend(queries[index][None], keys[index][None], values[index][None], parent[None], path[None], state[None], rates)
        return (attn[0], fresh[0])
    attn_rows, new_states = lax.map(one_row, (held, states, parents, path_nodes))
    attn = attn_rows[jnp.argsort(held)]
    attn_wide = attn.astype(jnp.float32)
    mean_square = lax.optimization_barrier(jnp.mean(attn_wide * attn_wide, axis=-1, keepdims=True))
    mixed = (attn_wide * lax.rsqrt(mean_square + EPS) * gain).astype(jnp.bfloat16)
    return (mixed, new_states)
```

```python
import functools

import jax
import jax.numpy as jnp
from jax import lax
from jax.experimental import pallas as pl
from jax.experimental.pallas import tpu as pltpu
from jax.sharding import PartitionSpec as P

HEADS = 64
HD = 128
NODES = 64
EPS = 1e-06
F32 = jnp.float32
BF16 = jnp.bfloat16


def dot(a, b, dims=((1,), (0,))):
    return lax.dot_general(a, b, (dims, ((), ())), preferred_element_type=F32)


def cast_kernel(rows, dest_ref, states_ref, out_ref, wide, narrow, in_sem, out_sem):
    def fetch(j):
        return pltpu.make_async_copy(states_ref.at[j], wide.at[j], in_sem.at[j])

    def store(j):
        return pltpu.make_async_copy(narrow.at[j], out_ref.at[dest_ref[j]], out_sem.at[j])

    for j in range(rows):
        fetch(j).start()
    for j in range(rows):
        fetch(j).wait()
        narrow[j] = wide[j].astype(BF16)
        store(j).start()
    for j in range(rows):
        store(j).wait()


def cast_states(dest, states):
    rows, height, width = states.shape
    return pl.pallas_call(
        functools.partial(cast_kernel, rows),
        out_shape=jax.ShapeDtypeStruct(states.shape, BF16),
        in_specs=[
            pl.BlockSpec(memory_space=pltpu.SMEM),
            pl.BlockSpec(memory_space=pl.ANY),
        ],
        out_specs=pl.BlockSpec(memory_space=pl.ANY),
        scratch_shapes=[
            pltpu.VMEM(states.shape, F32),
            pltpu.VMEM(states.shape, BF16),
            pltpu.SemaphoreType.DMA((rows,)),
            pltpu.SemaphoreType.DMA((rows,)),
        ],
        compiler_params=pltpu.CompilerParams(vmem_limit_bytes=24 << 20),
        cost_estimate=pl.CostEstimate(flops=0, bytes_accessed=states.size * 6, transcendentals=0),
        name="cast_states",
    )(dest, states)


def tree_kernel(
    heads, ids_ref, pos_ref, rates_ref, tree_ref, q_ref, k_ref, v_ref, local_ref, update_ref, depth_ref
):
    tree = tree_ref[0]
    parents = tree[:, :NODES]
    path = tree[:, NODES:]
    row = lax.broadcasted_iota(jnp.int32, (NODES, NODES), 0)
    col = lax.broadcasted_iota(jnp.int32, (NODES, NODES), 1)
    step = (jnp.broadcast_to(parents, (NODES, NODES)) == row).astype(F32).astype(BF16)
    reach_t = (row == col).astype(F32) + step.astype(F32)
    hops = 2
    while hops < NODES:
        step = dot(step, step).astype(BF16)
        reach_t = reach_t + dot(step, reach_t.astype(BF16))
        hops *= 2
    depth_row = jnp.sum(reach_t, axis=0, keepdims=True)
    reach = reach_t.T
    depth = jnp.sum(reach, axis=1, keepdims=True)
    spacing = jnp.maximum(depth - depth_row, 0.0)
    onpath = jnp.sum(
        (jnp.broadcast_to(path, (NODES, NODES)) == row).astype(F32), axis=1, keepdims=True
    )
    length = jnp.sum((path >= 0).astype(F32), axis=1, keepdims=True)
    depth_ref[0] = jnp.broadcast_to(depth, (NODES, HD))
    for h in range(heads):
        at = slice(h * HD, (h + 1) * HD)
        rate = rates_ref[h]
        q, k, v = q_ref[0, :, at], k_ref[0, :, at], v_ref[0, :, at]
        fading = jnp.exp(-rate * spacing) * reach
        weights = (dot(q, k, ((1,), (1,))) * fading).astype(BF16)
        local_ref[0, :, at] = dot(weights, v)
        path_weight = onpath * jnp.exp(-rate * (length - depth))
        scaled = v.astype(F32) * path_weight
        high = scaled.astype(BF16)
        low = (scaled - high.astype(F32)).astype(BF16)
        update = dot(k, high, ((0,), (0,))) + dot(k, low, ((0,), (0,)))
        update_ref[0, at, :] = update.astype(BF16)


def tree_part(ids, pos, rates, trees, queries, keys, values):
    rows, nodes, width = queries.shape
    heads = width // HD
    token = pl.BlockSpec((1, nodes, width), lambda s, ids, pos: (ids[s], 0, 0))
    return pl.pallas_call(
        functools.partial(tree_kernel, heads),
        out_shape=(
            jax.ShapeDtypeStruct((rows, nodes, width), F32),
            jax.ShapeDtypeStruct((rows, width, HD), BF16),
            jax.ShapeDtypeStruct((rows, nodes, HD), F32),
        ),
        grid_spec=pltpu.PrefetchScalarGridSpec(
            num_scalar_prefetch=2,
            grid=(rows,),
            in_specs=[
                pl.BlockSpec(memory_space=pltpu.SMEM),
                pl.BlockSpec((1, 1, 2 * nodes), lambda s, ids, pos: (pos[s], 0, 0)),
                token,
                token,
                token,
            ],
            out_specs=[
                pl.BlockSpec((1, nodes, width), lambda s, ids, pos: (s, 0, 0)),
                pl.BlockSpec((1, width, HD), lambda s, ids, pos: (s, 0, 0)),
                pl.BlockSpec((1, nodes, HD), lambda s, ids, pos: (s, 0, 0)),
            ],
        ),
        compiler_params=pltpu.CompilerParams(vmem_limit_bytes=24 << 20),
        cost_estimate=pl.CostEstimate(
            flops=rows * heads * 2 * 64 * 128 * 400,
            bytes_accessed=rows * nodes * width * 14,
            transcendentals=rows * heads * 4096,
        ),
        name="tree_part",
    )(ids, pos, rates, trees, queries, keys, values)


def prior_kernel(heads, ids_ref, rates_ref, q_ref, state_ref, local_ref, depth_ref, attn_ref, square_ref):
    depth = depth_ref[0]
    total = jnp.zeros((NODES, HD), F32)
    for h in range(heads):
        at = slice(h * HD, (h + 1) * HD)
        prior = dot(q_ref[0, :, at], state_ref[0, at, :])
        attn = (local_ref[0, :, at] + prior * jnp.exp(-rates_ref[h] * depth)).astype(BF16)
        attn_ref[0, :, at] = attn
        wide = attn.astype(F32)
        total = total + wide * wide
    square_ref[0] = jnp.sum(total.T, axis=0, keepdims=True)


def prior_part(ids, rates, queries, states, local, depth):
    rows, nodes, width = queries.shape
    heads = width // HD
    return pl.pallas_call(
        functools.partial(prior_kernel, heads),
        out_shape=(
            jax.ShapeDtypeStruct((rows, nodes, width), BF16),
            jax.ShapeDtypeStruct((rows, 1, nodes), F32),
        ),
        grid_spec=pltpu.PrefetchScalarGridSpec(
            num_scalar_prefetch=1,
            grid=(rows,),
            in_specs=[
                pl.BlockSpec(memory_space=pltpu.SMEM),
                pl.BlockSpec((1, nodes, width), lambda s, ids: (ids[s], 0, 0)),
                pl.BlockSpec((1, width, HD), lambda s, ids: (s, 0, 0)),
                pl.BlockSpec((1, nodes, width), lambda s, ids: (s, 0, 0)),
                pl.BlockSpec((1, nodes, HD), lambda s, ids: (s, 0, 0)),
            ],
            out_specs=[
                pl.BlockSpec((1, nodes, width), lambda s, ids: (ids[s], 0, 0)),
                pl.BlockSpec((1, 1, nodes), lambda s, ids: (ids[s], 0, 0)),
            ],
        ),
        compiler_params=pltpu.CompilerParams(vmem_limit_bytes=24 << 20),
        cost_estimate=pl.CostEstimate(
            flops=rows * heads * 2 * 64 * 128 * 128,
            bytes_accessed=rows * nodes * width * 12,
            transcendentals=rows * heads * 8192,
        ),
        name="prior_part",
    )(ids, rates, queries, states, local, depth)


def norm_kernel(attn_ref, square_ref, gain_ref, mixed_ref):
    scale = lax.rsqrt(square_ref[0] / (HEADS * HD) + EPS)
    scale = jnp.broadcast_to(scale, (HD, NODES)).T
    width = attn_ref.shape[-1]
    for h in range(width // HD):
        at = slice(h * HD, (h + 1) * HD)
        mixed_ref[0, :, at] = (attn_ref[0, :, at].astype(F32) * scale * gain_ref[:, at]).astype(BF16)


def normalize(attn, square, gain):
    rows, nodes, width = attn.shape
    return pl.pallas_call(
        norm_kernel,
        out_shape=jax.ShapeDtypeStruct(attn.shape, BF16),
        grid=(rows,),
        in_specs=[
            pl.BlockSpec((1, nodes, width), lambda r: (r, 0, 0)),
            pl.BlockSpec((1, 1, nodes), lambda r: (r, 0, 0)),
            pl.BlockSpec((1, width), lambda r: (0, 0)),
        ],
        out_specs=pl.BlockSpec((1, nodes, width), lambda r: (r, 0, 0)),
        cost_estimate=pl.CostEstimate(
            flops=attn.size * 2, bytes_accessed=attn.size * 4, transcendentals=0
        ),
        name="normalize",
    )(attn, square, gain)


def fresh_kernel(
    rows, dest_ref, leading_ref, states_ref, update_ref, out_ref, state, update, fresh, in_sem, up_sem, out_sem
):
    heads = state.shape[1] // HD

    def fetch(j):
        return pltpu.make_async_copy(states_ref.at[j], state.at[j], in_sem.at[j])

    def fetch_update(j):
        return pltpu.make_async_copy(update_ref.at[dest_ref[j]], update.at[j], up_sem.at[j])

    def store(j):
        return pltpu.make_async_copy(fresh.at[j], out_ref.at[j], out_sem.at[j])

    for j in range(rows):
        fetch(j).start()
        fetch_update(j).start()
    for j in range(rows):
        fetch(j).wait()
        fetch_update(j).wait()
        for h in range(heads):
            at = slice(h * HD, (h + 1) * HD)
            fresh[j, at, :] = leading_ref[j, h] * state[j, at, :] + update[j, at, :].astype(F32)
        store(j).start()
    for j in range(rows):
        store(j).wait()


def fresh_states(dest, leading, states, update):
    rows = states.shape[0]
    return pl.pallas_call(
        functools.partial(fresh_kernel, rows),
        out_shape=jax.ShapeDtypeStruct(states.shape, F32),
        in_specs=[
            pl.BlockSpec(memory_space=pltpu.SMEM),
            pl.BlockSpec(memory_space=pltpu.SMEM),
            pl.BlockSpec(memory_space=pl.ANY),
            pl.BlockSpec(memory_space=pl.ANY),
        ],
        out_specs=pl.BlockSpec(memory_space=pl.ANY),
        scratch_shapes=[
            pltpu.VMEM(states.shape, F32),
            pltpu.VMEM(states.shape, BF16),
            pltpu.VMEM(states.shape, F32),
            pltpu.SemaphoreType.DMA((rows,)),
            pltpu.SemaphoreType.DMA((rows,)),
            pltpu.SemaphoreType.DMA((rows,)),
        ],
        compiler_params=pltpu.CompilerParams(vmem_limit_bytes=32 << 20),
        cost_estimate=pl.CostEstimate(
            flops=states.size * 2, bytes_accessed=states.size * 10, transcendentals=0
        ),
        name="fresh_states",
    )(dest, leading, states, update)


def body(queries, keys, values, states, parents, path_nodes, held, rates, gain):
    req_count = lax.axis_size("req")
    req_rank = lax.axis_index("req")
    rows, nodes, width = queries.shape
    heads = width // HD
    flat_states = states.reshape(rows, width, HD)

    table = held.reshape(req_count, rows)
    dest = lax.dynamic_index_in_dim(table, req_rank, 0, keepdims=False) // rows
    hit = table // rows == req_rank
    place = lax.broadcasted_iota(jnp.int32, table.shape, 0) * rows + lax.broadcasted_iota(
        jnp.int32, table.shape, 1
    )
    ids = jnp.sum(jnp.where(hit, table - req_rank * rows, 0), axis=1)
    pos = jnp.sum(jnp.where(hit, place, 0), axis=1)

    trees = lax.all_gather(
        jnp.concatenate([parents, path_nodes], axis=1), "req", axis=0, tiled=True
    )
    sent = cast_states(dest, flat_states)
    arrived = lax.all_to_all(sent, "req", split_axis=0, concat_axis=0, tiled=True)
    local, update, depth = tree_part(
        ids, pos, rates, trees.reshape(req_count * rows, 1, 2 * nodes), queries, keys, values
    )
    update_back = lax.all_to_all(update, "req", split_axis=0, concat_axis=0, tiled=True)
    attn, square = prior_part(ids, rates, queries, arrived, local, depth)
    total = lax.psum(square.reshape(rows, nodes), "head")
    mixed = normalize(attn, total.reshape(rows, 1, nodes), gain.reshape(1, width))

    length = jnp.sum((path_nodes >= 0).astype(F32), axis=1)
    leading = jnp.exp(-rates[None, :] * length[:, None])
    fresh = fresh_states(dest, leading, flat_states, update_back)
    return (mixed, fresh.reshape(rows, heads, HD, HD))


def solution(mesh):
    in_specs = (
        P("req", None, "head"),
        P("req", None, "head"),
        P("req", None, "head"),
        P("req", "head", None, None),
        P("req", None),
        P("req", None),
        P(),
        P("head"),
        P("head"),
    )
    out_specs = (P("req", None, "head"), P("req", "head", None, None))
    return jax.shard_map(body, mesh=mesh, in_specs=in_specs, out_specs=out_specs, check_vma=False)
```

```python
import functools

import jax
import jax.numpy as jnp
from jax import lax
from jax.experimental import pallas as pl
from jax.experimental.pallas import tpu as pltpu
from jax.sharding import PartitionSpec as P

HEADS = 64
HD = 128
NODES = 64
EPS = 1e-06
F32 = jnp.float32
BF16 = jnp.bfloat16
TAIL = 16
FAR = 1e30
EARLY = 3
VMEM_LIMIT = 56 << 20
HBM = pl.BlockSpec(memory_space=pltpu.HBM)
SMEM = pl.BlockSpec(memory_space=pltpu.SMEM)
VMEM = pl.BlockSpec(memory_space=pltpu.VMEM)
PARAMS = pltpu.CompilerParams(vmem_limit_bytes=VMEM_LIMIT)


def dot(a, b, dims=((1,), (0,))):
    return lax.dot_general(a, b, (dims, ((), ())), preferred_element_type=F32)


def cost(bytes_accessed, flops=0, transcendentals=0):
    return pl.CostEstimate(
        flops=int(flops), bytes_accessed=int(bytes_accessed), transcendentals=int(transcendentals)
    )


def path_weights(path):
    entry = jnp.broadcast_to(path, (NODES, NODES))
    row = lax.broadcasted_iota(jnp.int32, (NODES, NODES), 0).astype(F32)
    place = lax.broadcasted_iota(jnp.int32, (1, NODES), 1).astype(F32)
    length = jnp.sum((path >= 0.0).astype(F32), axis=1, keepdims=True)
    match = (entry == row).astype(F32)
    onpath = jnp.sum(match, axis=1, keepdims=True)
    age = jnp.sum(match * (length - 1.0 - place), axis=1, keepdims=True)
    return length, jnp.broadcast_to(onpath, (NODES, HD)), jnp.broadcast_to(age, (NODES, HD))


def diagonal(a, b):
    zero = jnp.zeros(a.shape, a.dtype)
    return jnp.concatenate(
        [jnp.concatenate([a, zero], axis=1), jnp.concatenate([zero, b], axis=1)], axis=0
    )


def parts(v, weight):
    scaled = v.astype(F32) * weight
    high = scaled.astype(BF16)
    return high, (scaled - high.astype(F32)).astype(BF16)


def outer(keys, values, weights):
    split = [parts(v, weight) for v, weight in zip(values, weights)]
    if len(keys) == 1:
        both = dot(keys[0], jnp.concatenate(split[0], axis=1), ((0,), (0,)))
        return both[:, :HD] + both[:, HD:]
    stacked = jnp.concatenate(keys + keys, axis=0)
    spread = [diagonal(split[0][at], split[1][at]) for at in (0, 1)]
    return dot(stacked, jnp.concatenate(spread, axis=0), ((0,), (0,)))


def pack_kernel(
    rows, heads, me_ref, held_ref, parents_ref, path_ref, states_ref, keys_ref, values_ref,
    early_ref, late_ref, dest_ref, ids_ref,
    wide, k_all, v_all, early, late, in_sem, out_sem,
):
    height = wide.shape[1]

    def fetch(j):
        return pltpu.make_async_copy(states_ref.at[j], wide.at[j], in_sem.at[3 * j])

    def fetch_pair(j):
        at = ids_ref[dest_ref[j]]
        return (
            pltpu.make_async_copy(keys_ref.at[at], k_all.at[j], in_sem.at[3 * j + 1]),
            pltpu.make_async_copy(values_ref.at[at], v_all.at[j], in_sem.at[3 * j + 2]),
        )

    def store(j):
        return (
            pltpu.make_async_copy(early.at[j], early_ref.at[dest_ref[j]], out_sem.at[2 * j]),
            pltpu.make_async_copy(late.at[j], late_ref.at[dest_ref[j]], out_sem.at[2 * j + 1]),
        )

    for j in range(rows):
        fetch(j).start()
    me = me_ref[0]
    for j in range(rows):
        dest_ref[j] = lax.div(held_ref[me * rows + j], rows)
    for s in range(held_ref.shape[0] // rows):
        found = 0
        for i in range(rows):
            request = held_ref[s * rows + i]
            found = jnp.where(lax.div(request, rows) == me, request - me * rows, found)
        ids_ref[s] = found
    for j in range(rows):
        for copy in fetch_pair(j):
            copy.start()

    def work(j, carry):
        fetch(j).wait()
        for copy in fetch_pair(j):
            copy.wait()
        early[j, :height, :] = wide[j].astype(BF16)
        for h in range(heads):
            at = slice(h * HD, (h + 1) * HD)
            base, ref = (height, early) if h < EARLY else (0, late)
            count = EARLY if h < EARLY else heads - EARLY
            h -= 0 if h < EARLY else EARLY
            ref[j, base + h * NODES : base + (h + 1) * NODES, :] = k_all[j, :, at]
            base += count * NODES
            ref[j, base + h * NODES : base + (h + 1) * NODES, :] = v_all[j, :, at]
        both = jnp.concatenate(
            [parents_ref[pl.ds(j, 1), :], path_ref[pl.ds(j, 1), :]], axis=1
        ).astype(F32)
        early[j, height + 2 * EARLY * NODES :, :] = jnp.broadcast_to(both, (TAIL, HD)).astype(BF16)
        for copy in store(j):
            copy.start()
        return carry

    lax.fori_loop(0, rows, work, 0)
    for j in range(rows):
        for copy in store(j):
            copy.wait()


def pack(me, held, parents, path_nodes, states, keys, values):
    rows, height, width = states.shape
    nodes = keys.shape[1]
    heads = height // HD
    early = (rows, height + 2 * EARLY * nodes + TAIL, width)
    late = (rows, 2 * (heads - EARLY) * nodes, width)
    return pl.pallas_call(
        functools.partial(pack_kernel, rows, heads),
        out_shape=(
            jax.ShapeDtypeStruct(early, BF16),
            jax.ShapeDtypeStruct(late, BF16),
            jax.ShapeDtypeStruct((rows,), jnp.int32),
            jax.ShapeDtypeStruct((held.shape[0] // rows,), jnp.int32),
        ),
        in_specs=[SMEM, SMEM, VMEM, VMEM, HBM, HBM, HBM],
        out_specs=(HBM, HBM, SMEM, SMEM),
        scratch_shapes=[
            pltpu.VMEM(states.shape, F32),
            pltpu.VMEM(keys.shape, BF16),
            pltpu.VMEM(keys.shape, BF16),
            pltpu.VMEM(early, BF16),
            pltpu.VMEM(late, BF16),
            pltpu.SemaphoreType.DMA((3 * rows,)),
            pltpu.SemaphoreType.DMA((2 * rows,)),
        ],
        compiler_params=PARAMS,
        cost_estimate=cost(20e6),
        name="pack",
    )(me, held, parents, path_nodes, states, keys, values)


def gate_kernel(value_ref, after_ref, out_ref):
    pass


def gate(value, after):
    return pl.pallas_call(
        gate_kernel,
        out_shape=jax.ShapeDtypeStruct(value.shape, value.dtype),
        in_specs=[HBM, HBM],
        out_specs=HBM,
        input_output_aliases={0: 0},
        compiler_params=PARAMS,
        cost_estimate=cost(1000),
        name="gate",
    )(value, after)


def attend_kernel(
    rows, heads, ids_ref, rates_ref, early_ref, q_hbm, k_hbm, v_hbm, attn_ref, square_ref,
    q_all, k_all, v_all, state_all, tails, gaps, depths, weights, sem, tail_sem,
):
    tail = early_ref.shape[1] - TAIL
    height = state_all.shape[1]
    tail_copy = pltpu.make_async_copy(early_ref.at[:, pl.ds(tail, TAIL), :], tails, tail_sem)

    def copies(s):
        at = ids_ref[s]
        return (
            pltpu.make_async_copy(q_hbm.at[at], q_all.at[s], sem.at[4 * s]),
            pltpu.make_async_copy(k_hbm.at[at], k_all.at[s], sem.at[4 * s + 1]),
            pltpu.make_async_copy(v_hbm.at[at], v_all.at[s], sem.at[4 * s + 2]),
            pltpu.make_async_copy(
                early_ref.at[s, pl.ds(0, height), :], state_all.at[s], sem.at[4 * s + 3]
            ),
        )

    tail_copy.start()
    for s in range(rows):
        for copy in copies(s):
            copy.start()
    tail_copy.wait()

    row = lax.broadcasted_iota(jnp.int32, (NODES, NODES), 0)
    col = lax.broadcasted_iota(jnp.int32, (NODES, NODES), 1)
    row_wide = row.astype(F32)
    eye = (row == col).astype(F32)
    batch = 4

    def grow(group, carry):
        steps, reaches = [], []
        for b in range(batch):
            parents = tails[group * batch + b].astype(F32)[0:1, :NODES]
            step = (jnp.broadcast_to(parents, (NODES, NODES)) == row_wide).astype(F32)
            steps.append(step.astype(BF16))
            reaches.append(eye + step)
        hops = 2
        while hops < NODES:
            steps = [dot(x, x).astype(BF16) for x in steps]
            reaches = [r + dot(x, r.astype(BF16)) for x, r in zip(steps, reaches)]
            hops *= 2
        for b in range(batch):
            s = group * batch + b
            reach = reaches[b].T
            depth_row = jnp.sum(reaches[b], axis=0, keepdims=True)
            depth = jnp.sum(reach, axis=1, keepdims=True)
            gap = jnp.where(reach > 0.5, depth - depth_row, FAR)
            gaps[s] = jnp.concatenate([gap, gap], axis=1)
            depths[s] = jnp.broadcast_to(depth, (NODES, HD))
        return carry

    lax.fori_loop(0, rows // batch, grow, 0)

    lane = lax.broadcasted_iota(jnp.int32, (1, HD), 1)

    def score(s, carry):
        for copy in copies(s):
            copy.wait()
        gap = gaps[s]
        for pair in range(heads // 2):
            a = slice(2 * pair * HD, (2 * pair + 1) * HD)
            b = slice((2 * pair + 1) * HD, (2 * pair + 2) * HD)
            q = q_all[s, :, 2 * pair * HD : (2 * pair + 2) * HD]
            scores = dot(q, diagonal(k_all[s, :, a], k_all[s, :, b]), ((1,), (1,)))
            rate = jnp.where(lane < NODES, rates_ref[2 * pair], rates_ref[2 * pair + 1])
            weights[s, pair] = (scores * jnp.exp(-rate * gap)).astype(BF16)
        return carry

    def finish(s, carry):
        depth = depths[s]
        at_row = ids_ref[s]
        total = jnp.zeros((NODES, HD), F32)
        for pair in range(heads // 2):
            a = slice(2 * pair * HD, (2 * pair + 1) * HD)
            b = slice((2 * pair + 1) * HD, (2 * pair + 2) * HD)
            q = q_all[s, :, 2 * pair * HD : (2 * pair + 2) * HD]
            local = dot(weights[s, pair], diagonal(v_all[s, :, a], v_all[s, :, b]))
            prior = dot(q, diagonal(state_all[s, a, :], state_all[s, b, :]))
            for h, at, cut in ((2 * pair, a, slice(0, HD)), (2 * pair + 1, b, slice(HD, 2 * HD))):
                decay = jnp.exp(-rates_ref[h] * depth)
                attn = (local[:, cut] + prior[:, cut] * decay).astype(BF16)
                attn_ref[at_row, :, at] = attn
                wide = attn.astype(F32)
                total = total + wide * wide
        square_ref[pl.ds(at_row, 1), :] = jnp.sum(total.T, axis=0, keepdims=True)
        return carry

    lax.fori_loop(0, rows, score, 0)
    lax.fori_loop(0, rows, finish, 0, unroll=2)


def attend(ids, rates, early, queries, keys, values):
    rows, nodes, width = queries.shape
    return pl.pallas_call(
        functools.partial(attend_kernel, rows, width // HD),
        out_shape=(
            jax.ShapeDtypeStruct((rows, nodes, width), BF16),
            jax.ShapeDtypeStruct((rows, nodes), F32),
        ),
        in_specs=[SMEM, SMEM, HBM, HBM, HBM, HBM],
        out_specs=(VMEM, VMEM),
        scratch_shapes=[
            pltpu.VMEM((rows, nodes, width), BF16),
            pltpu.VMEM((rows, nodes, width), BF16),
            pltpu.VMEM((rows, nodes, width), BF16),
            pltpu.VMEM((rows, width, HD), BF16),
            pltpu.VMEM((rows, TAIL, HD), BF16),
            pltpu.VMEM((rows, nodes, 2 * nodes), F32),
            pltpu.VMEM((rows, nodes, HD), F32),
            pltpu.VMEM((rows, width // HD // 2, nodes, 2 * nodes), BF16),
            pltpu.SemaphoreType.DMA((4 * rows,)),
            pltpu.SemaphoreType.DMA,
        ],
        compiler_params=PARAMS,
        cost_estimate=cost(50e6, 1e9),
        name="attend",
    )(ids, rates, early, queries, keys, values)


def update_kernel(
    rows, first, heads, base, dest_ref, rates_ref, path_ref, states_ref, pairs_ref, *refs
):
    out_ref, state, fresh, pair, onpaths, ages, lengths, in_sem, pair_sem, out_sem = refs[-10:]
    direct = pair.shape[0] == 1
    part = pl.ds(first * HD, heads * HD)

    def fetch(j):
        copies = [pltpu.make_async_copy(states_ref.at[j, part, :], state.at[j], in_sem.at[j])]
        if not direct:
            source = pairs_ref.at[dest_ref[j], pl.ds(base, 2 * heads * NODES), :]
            copies.append(pltpu.make_async_copy(source, pair.at[j], pair_sem.at[j]))
        return copies

    def store(j):
        return pltpu.make_async_copy(fresh.at[j], out_ref.at[j, part, :], out_sem.at[j])

    for j in range(rows):
        for copy in fetch(j):
            copy.start()

    for j in range(rows):
        length, onpath, age = path_weights(path_ref[j : j + 1, :].astype(F32))
        onpaths[j], ages[j] = onpath, age
        lengths[j] = jnp.broadcast_to(length, (8, HD))

    def work(j, carry):
        onpath, age, length = onpaths[j], ages[j], lengths[j, 0:1, :]
        for copy in fetch(j):
            copy.wait()
        ready, row = (pairs_ref, dest_ref[j]) if direct else (pair, j)
        for start in range(0, heads, 2):
            group = range(start, min(start + 2, heads))
            update = outer(
                [ready[row, h * NODES : (h + 1) * NODES, :] for h in group],
                [ready[row, (heads + h) * NODES : (heads + h + 1) * NODES, :] for h in group],
                [onpath * jnp.exp(-rates_ref[first + h] * age) for h in group],
            )
            for n, h in enumerate(group):
                at = slice(h * HD, (h + 1) * HD)
                kept = jnp.exp(-rates_ref[first + h] * length) * state[j, at, :]
                fresh[j, at, :] = kept + update[:, n * HD : (n + 1) * HD]
        store(j).start()
        return carry

    lax.fori_loop(0, rows, work, 0, unroll=2)
    for j in range(rows):
        store(j).wait()


def update_states(first, heads, base, dest, rates, path_nodes, states, pairs, partial):
    rows, _, width = states.shape
    earlier = [] if partial is None else [partial]
    direct = pairs.shape[1] == 2 * heads * NODES
    return pl.pallas_call(
        functools.partial(update_kernel, rows, first, heads, base),
        out_shape=jax.ShapeDtypeStruct(states.shape, F32),
        in_specs=[SMEM, SMEM, VMEM, HBM, VMEM if direct else HBM] + [HBM] * len(earlier),
        out_specs=HBM,
        input_output_aliases={5: 0} if earlier else {},
        scratch_shapes=[
            pltpu.VMEM((rows, heads * HD, width), F32),
            pltpu.VMEM((rows, heads * HD, width), F32),
            pltpu.VMEM((1 if direct else rows, 2 * heads * NODES, HD), BF16),
            pltpu.VMEM((rows, NODES, HD), F32),
            pltpu.VMEM((rows, NODES, HD), F32),
            pltpu.VMEM((rows, 8, HD), F32),
            pltpu.SemaphoreType.DMA((rows,)),
            pltpu.SemaphoreType.DMA((rows,)),
            pltpu.SemaphoreType.DMA((rows,)),
        ],
        compiler_params=pltpu.CompilerParams(vmem_limit_bytes=(49 if direct else 56) << 20),
        cost_estimate=cost(10e6, 5e8),
        name="update_states",
    )(dest, rates, path_nodes, states, pairs, *earlier)


def body(queries, keys, values, states, parents, path_nodes, held, rates, gain):
    me = lax.axis_index("req")
    rows, nodes, width = queries.shape
    heads = width // HD
    flat_states = states.reshape(rows, width, HD)

    def swap(x):
        return lax.all_to_all(x, "req", split_axis=0, concat_axis=0, tiled=True)

    early, late, dest, ids = pack(
        me.reshape(1), held, parents, path_nodes, flat_states, keys, values
    )
    early = swap(early)
    late = swap(gate(late, early))
    attn, square = attend(ids, rates, early, queries, keys, values)
    fresh = update_states(0, EARLY, width, dest, rates, path_nodes, flat_states, early, None)
    head_count = lax.axis_size("head")
    square = square + lax.ppermute(square, "head", [(i, i ^ 1) for i in range(head_count)])
    others = [
        lax.ppermute(square, "head", [(i, (i + step) % head_count) for i in range(head_count)])
        for step in range(2, head_count, 2)
    ]
    square = square + sum(others)
    scaling = lax.rsqrt(square / (HEADS * HD) + EPS)
    mixed = (attn.astype(F32) * scaling[:, :, None] * gain).astype(BF16)
    fresh = update_states(
        EARLY, heads - EARLY, 0, dest, rates, path_nodes, flat_states, late, fresh
    )
    return (mixed, fresh.reshape(rows, heads, HD, HD))


def solution(mesh):
    in_specs = (
        P("req", None, "head"),
        P("req", None, "head"),
        P("req", None, "head"),
        P("req", "head", None, None),
        P("req", None),
        P("req", None),
        P(),
        P("head"),
        P("head"),
    )
    out_specs = (P("req", None, "head"), P("req", "head", None, None))
    return jax.shard_map(body, mesh=mesh, in_specs=in_specs, out_specs=out_specs, check_vma=False)
```

```python
import functools

import jax
import jax.numpy as jnp
from jax import lax
from jax.experimental import pallas as pl
from jax.experimental.pallas import tpu as pltpu
from jax.sharding import PartitionSpec as P

HEADS = 64
HD = 128
NODES = 64
EPS = 1e-06
F32 = jnp.float32
BF16 = jnp.bfloat16
TAIL = 16
FAR = 1e30
EARLY = 4
VMEM_LIMIT = 56 << 20
HBM = pl.BlockSpec(memory_space=pltpu.HBM)
SMEM = pl.BlockSpec(memory_space=pltpu.SMEM)
VMEM = pl.BlockSpec(memory_space=pltpu.VMEM)
PARAMS = pltpu.CompilerParams(vmem_limit_bytes=VMEM_LIMIT)


def dot(a, b, dims=((1,), (0,))):
    return lax.dot_general(a, b, (dims, ((), ())), preferred_element_type=F32)


def cost(bytes_accessed, flops=0, transcendentals=0):
    return pl.CostEstimate(
        flops=int(flops), bytes_accessed=int(bytes_accessed), transcendentals=int(transcendentals)
    )


def path_weights(path, length):
    row = lax.broadcasted_iota(jnp.int32, (NODES, NODES), 0)
    match = (jnp.broadcast_to(path, (NODES, NODES)) == row).astype(F32).astype(BF16)
    place = lax.broadcasted_iota(jnp.int32, (NODES, HD), 0).astype(F32)
    ages = jnp.maximum(length - 1.0 - place, 0.0).astype(BF16)
    both = dot(match, jnp.concatenate([jnp.ones((NODES, HD), BF16), ages], axis=1))
    return both[:, :HD], both[:, HD:]


def diagonal(a, b):
    zero = jnp.zeros(a.shape, a.dtype)
    return jnp.concatenate(
        [jnp.concatenate([a, zero], axis=1), jnp.concatenate([zero, b], axis=1)], axis=0
    )


def parts(v, weight):
    scaled = v.astype(F32) * weight
    high = scaled.astype(BF16)
    return high, (scaled - high.astype(F32)).astype(BF16)


def outer(keys, values, weights):
    split = [parts(v, weight) for v, weight in zip(values, weights)]
    if len(keys) == 1:
        both = dot(keys[0], jnp.concatenate(split[0], axis=1), ((0,), (0,)))
        return both[:, :HD] + both[:, HD:]
    stacked = jnp.concatenate(keys + keys, axis=0)
    spread = [diagonal(split[0][at], split[1][at]) for at in (0, 1)]
    return dot(stacked, jnp.concatenate(spread, axis=0), ((0,), (0,)))


def pack_kernel(
    rows, heads, me_ref, held_hbm, parents_hbm, path_hbm, states_ref, keys_ref, values_ref,
    early_ref, late_ref, dest_hbm, ids_hbm,
    wide, k_all, v_all, early, late, held_ref, parents_ref, path_ref, dest_ref, ids_ref, in_sem, out_sem, small_sem,
):
    height = wide.shape[1]

    def fetch(j):
        return pltpu.make_async_copy(states_ref.at[j], wide.at[j], in_sem.at[3 * j])

    def fetch_pair(j):
        at = ids_ref[dest_ref[j]]
        return (
            pltpu.make_async_copy(keys_ref.at[at], k_all.at[j], in_sem.at[3 * j + 1]),
            pltpu.make_async_copy(values_ref.at[at], v_all.at[j], in_sem.at[3 * j + 2]),
        )

    def store(j):
        return (
            pltpu.make_async_copy(early.at[j], early_ref.at[dest_ref[j]], out_sem.at[2 * j]),
            pltpu.make_async_copy(late.at[j], late_ref.at[dest_ref[j]], out_sem.at[2 * j + 1]),
        )

    held_copy = pltpu.make_async_copy(held_hbm, held_ref, small_sem.at[0])
    tree_copies = (
        pltpu.make_async_copy(parents_hbm, parents_ref, small_sem.at[1]),
        pltpu.make_async_copy(path_hbm, path_ref, small_sem.at[2]),
    )
    index_copies = (
        pltpu.make_async_copy(dest_ref, dest_hbm, small_sem.at[3]),
        pltpu.make_async_copy(ids_ref, ids_hbm, small_sem.at[4]),
    )
    held_copy.start()
    for copy in tree_copies:
        copy.start()
    for j in range(rows):
        fetch(j).start()
    held_copy.wait()
    me = me_ref[0]
    for j in range(rows):
        dest_ref[j] = lax.div(held_ref[me * rows + j], rows)
    for s in range(held_ref.shape[0] // rows):
        found = 0
        for i in range(rows):
            request = held_ref[s * rows + i]
            found = jnp.where(lax.div(request, rows) == me, request - me * rows, found)
        ids_ref[s] = found
    for j in range(rows):
        for copy in fetch_pair(j):
            copy.start()
    for copy in index_copies:
        copy.start()
    for copy in tree_copies:
        copy.wait()

    def work(j, carry):
        fetch(j).wait()
        for copy in fetch_pair(j):
            copy.wait()
        early[j, :height, :] = wide[j].astype(BF16)
        for h in range(heads):
            at = slice(h * HD, (h + 1) * HD)
            base, ref = (height, early) if h < EARLY else (0, late)
            count = EARLY if h < EARLY else heads - EARLY
            h -= 0 if h < EARLY else EARLY
            ref[j, base + h * NODES : base + (h + 1) * NODES, :] = k_all[j, :, at]
            base += count * NODES
            ref[j, base + h * NODES : base + (h + 1) * NODES, :] = v_all[j, :, at]
        both = jnp.concatenate(
            [parents_ref[pl.ds(j, 1), :], path_ref[pl.ds(j, 1), :]], axis=1
        ).astype(F32)
        early[j, height + 2 * EARLY * NODES :, :] = jnp.broadcast_to(both, (TAIL, HD)).astype(BF16)
        for copy in store(j):
            copy.start()
        return carry

    lax.fori_loop(0, rows, work, 0)
    for copy in index_copies:
        copy.wait()
    for j in range(rows):
        for copy in store(j):
            copy.wait()


def pack(me, held, parents, path_nodes, states, keys, values):
    rows, height, width = states.shape
    nodes = keys.shape[1]
    heads = height // HD
    early = (rows, height + 2 * EARLY * nodes + TAIL, width)
    late = (rows, 2 * (heads - EARLY) * nodes, width)
    return pl.pallas_call(
        functools.partial(pack_kernel, rows, heads),
        out_shape=(
            jax.ShapeDtypeStruct(early, BF16),
            jax.ShapeDtypeStruct(late, BF16),
            jax.ShapeDtypeStruct((rows,), jnp.int32),
            jax.ShapeDtypeStruct((held.shape[0] // rows,), jnp.int32),
        ),
        in_specs=[SMEM, HBM, HBM, HBM, HBM, HBM, HBM],
        out_specs=(HBM, HBM, HBM, HBM),
        scratch_shapes=[
            pltpu.VMEM(states.shape, F32),
            pltpu.VMEM(keys.shape, BF16),
            pltpu.VMEM(keys.shape, BF16),
            pltpu.VMEM(early, BF16),
            pltpu.VMEM(late, BF16),
            pltpu.SMEM(held.shape, jnp.int32),
            pltpu.VMEM(parents.shape, jnp.int32),
            pltpu.VMEM(path_nodes.shape, jnp.int32),
            pltpu.SMEM((rows,), jnp.int32),
            pltpu.SMEM((held.shape[0] // rows,), jnp.int32),
            pltpu.SemaphoreType.DMA((3 * rows,)),
            pltpu.SemaphoreType.DMA((2 * rows,)),
            pltpu.SemaphoreType.DMA((5,)),
        ],
        compiler_params=PARAMS,
        cost_estimate=cost(20e6),
        name="pack",
    )(me, held, parents, path_nodes, states, keys, values)


def gate_kernel(value_ref, after_ref, out_ref):
    pass


def gate(value, after):
    return pl.pallas_call(
        gate_kernel,
        out_shape=jax.ShapeDtypeStruct(value.shape, value.dtype),
        in_specs=[HBM, HBM],
        out_specs=HBM,
        input_output_aliases={0: 0},
        compiler_params=PARAMS,
        cost_estimate=cost(1000),
        name="gate",
    )(value, after)


def attend_kernel(
    rows, heads, ids_hbm, rates_hbm, early_ref, q_hbm, k_hbm, v_hbm, attn_ref, square_ref,
    q_all, k_all, v_all, state_all, tails, gaps, depths, weights, ids_ref, rates_ref, sem, tail_sem, small_sem,
):
    tail = early_ref.shape[1] - TAIL
    height = state_all.shape[1]
    tail_copy = pltpu.make_async_copy(early_ref.at[:, pl.ds(tail, TAIL), :], tails, tail_sem)

    def copies(s):
        at = ids_ref[s]
        return (
            pltpu.make_async_copy(q_hbm.at[at], q_all.at[s], sem.at[4 * s]),
            pltpu.make_async_copy(k_hbm.at[at], k_all.at[s], sem.at[4 * s + 1]),
            pltpu.make_async_copy(v_hbm.at[at], v_all.at[s], sem.at[4 * s + 2]),
            pltpu.make_async_copy(
                early_ref.at[s, pl.ds(0, height), :], state_all.at[s], sem.at[4 * s + 3]
            ),
        )

    ids_copy = pltpu.make_async_copy(ids_hbm, ids_ref, small_sem.at[0])
    rates_copy = pltpu.make_async_copy(rates_hbm, rates_ref, small_sem.at[1])
    ids_copy.start()
    rates_copy.start()
    tail_copy.start()
    ids_copy.wait()
    for s in range(rows):
        for copy in copies(s):
            copy.start()
    rates_copy.wait()
    tail_copy.wait()

    row = lax.broadcasted_iota(jnp.int32, (NODES, NODES), 0)
    col = lax.broadcasted_iota(jnp.int32, (NODES, NODES), 1)
    row_wide = row.astype(F32)
    eye = (row == col).astype(F32)
    batch = 4

    def grow(group, carry):
        steps, reaches = [], []
        for b in range(batch):
            parents = tails[group * batch + b].astype(F32)[0:1, :NODES]
            step = (jnp.broadcast_to(parents, (NODES, NODES)) == row_wide).astype(F32)
            steps.append(step.astype(BF16))
            reaches.append(eye + step)
        hops = 2
        while hops < NODES:
            steps = [dot(x, x).astype(BF16) for x in steps]
            reaches = [r + dot(x, r.astype(BF16)) for x, r in zip(steps, reaches)]
            hops *= 2
        for b in range(batch):
            s = group * batch + b
            reach = reaches[b].T
            depth_row = jnp.sum(reaches[b], axis=0, keepdims=True)
            depth = jnp.sum(reach, axis=1, keepdims=True)
            gap = jnp.where(reach > 0.5, depth - depth_row, FAR)
            gaps[s] = jnp.concatenate([gap, gap], axis=1)
            depths[s] = jnp.broadcast_to(depth, (NODES, HD))
        return carry

    lax.fori_loop(0, rows // batch, grow, 0)

    lane = lax.broadcasted_iota(jnp.int32, (1, HD), 1)

    def score(s, carry):
        for copy in copies(s):
            copy.wait()
        gap = gaps[s]
        for pair in range(heads // 2):
            a = slice(2 * pair * HD, (2 * pair + 1) * HD)
            b = slice((2 * pair + 1) * HD, (2 * pair + 2) * HD)
            q = q_all[s, :, 2 * pair * HD : (2 * pair + 2) * HD]
            scores = dot(q, diagonal(k_all[s, :, a], k_all[s, :, b]), ((1,), (1,)))
            rate = jnp.where(lane < NODES, rates_ref[2 * pair], rates_ref[2 * pair + 1])
            weights[s, pair] = (scores * jnp.exp(-rate * gap)).astype(BF16)
        return carry

    def finish(s, carry):
        depth = depths[s]
        at_row = ids_ref[s]
        total = jnp.zeros((NODES, HD), F32)
        for pair in range(heads // 2):
            a = slice(2 * pair * HD, (2 * pair + 1) * HD)
            b = slice((2 * pair + 1) * HD, (2 * pair + 2) * HD)
            q = q_all[s, :, 2 * pair * HD : (2 * pair + 2) * HD]
            local = dot(weights[s, pair], diagonal(v_all[s, :, a], v_all[s, :, b]))
            prior = dot(q, diagonal(state_all[s, a, :], state_all[s, b, :]))
            for h, at, cut in ((2 * pair, a, slice(0, HD)), (2 * pair + 1, b, slice(HD, 2 * HD))):
                decay = jnp.exp(-rates_ref[h] * depth)
                attn = (local[:, cut] + prior[:, cut] * decay).astype(BF16)
                attn_ref[at_row, :, at] = attn
                wide = attn.astype(F32)
                total = total + wide * wide
        square_ref[pl.ds(at_row, 1), :] = jnp.sum(total.T, axis=0, keepdims=True)
        return carry

    lax.fori_loop(0, rows, score, 0, unroll=2)
    lax.fori_loop(0, rows, finish, 0, unroll=2)


def attend(ids, rates, early, queries, keys, values):
    rows, nodes, width = queries.shape
    return pl.pallas_call(
        functools.partial(attend_kernel, rows, width // HD),
        out_shape=(
            jax.ShapeDtypeStruct((rows, nodes, width), BF16),
            jax.ShapeDtypeStruct((rows, nodes), F32),
        ),
        in_specs=[HBM, HBM, HBM, HBM, HBM, HBM],
        out_specs=(VMEM, VMEM),
        scratch_shapes=[
            pltpu.VMEM((rows, nodes, width), BF16),
            pltpu.VMEM((rows, nodes, width), BF16),
            pltpu.VMEM((rows, nodes, width), BF16),
            pltpu.VMEM((rows, width, HD), BF16),
            pltpu.VMEM((rows, TAIL, HD), BF16),
            pltpu.VMEM((rows, nodes, 2 * nodes), F32),
            pltpu.VMEM((rows, nodes, HD), F32),
            pltpu.VMEM((rows, width // HD // 2, nodes, 2 * nodes), BF16),
            pltpu.SMEM(ids.shape, jnp.int32),
            pltpu.SMEM(rates.shape, F32),
            pltpu.SemaphoreType.DMA((4 * rows,)),
            pltpu.SemaphoreType.DMA,
            pltpu.SemaphoreType.DMA((2,)),
        ],
        compiler_params=PARAMS,
        cost_estimate=cost(50e6, 1e9),
        name="attend",
    )(ids, rates, early, queries, keys, values)


def update_kernel(
    rows, first, heads, base, dest_hbm, rates_hbm, path_hbm, states_ref, pairs_ref, *refs
):
    out_ref, state, fresh, pair, onpaths, ages, lengths = refs[-14:-7]
    dest_ref, rates_ref, path_ref, in_sem, pair_sem, out_sem, small_sem = refs[-7:]
    direct = pair.shape[0] == 1
    part = pl.ds(first * HD, heads * HD)

    def fetch(j):
        copies = [pltpu.make_async_copy(states_ref.at[j, part, :], state.at[j], in_sem.at[j])]
        if not direct:
            source = pairs_ref.at[dest_ref[j], pl.ds(base, 2 * heads * NODES), :]
            copies.append(pltpu.make_async_copy(source, pair.at[j], pair_sem.at[j]))
        return copies

    def store(j):
        return pltpu.make_async_copy(fresh.at[j], out_ref.at[j, part, :], out_sem.at[j])

    small = [
        pltpu.make_async_copy(source, target, small_sem.at[n])
        for n, (source, target) in enumerate(
            ((dest_hbm, dest_ref), (path_hbm, path_ref), (rates_hbm, rates_ref))
        )
    ]
    for copy in small:
        copy.start()
    ahead = rows if direct else rows // 2
    if not direct:
        small[0].wait()
    for j in range(ahead):
        for copy in fetch(j):
            copy.start()
    for copy in small[0 if direct else 1 :]:
        copy.wait()

    counts = jnp.sum((path_ref[...] >= 0).astype(F32), axis=1, keepdims=True)
    counts = jnp.broadcast_to(counts, (rows, HD))
    for j in range(rows):
        length = counts[j : j + 1, :]
        onpaths[j], ages[j] = path_weights(path_ref[j : j + 1, :], length)
        lengths[j] = jnp.broadcast_to(length, (8, HD))
    for j in range(ahead, rows):
        for copy in fetch(j):
            copy.start()

    def work(j, carry):
        onpath, age, length = onpaths[j], ages[j], lengths[j, 0:1, :]
        for copy in fetch(j):
            copy.wait()
        ready, row = (pairs_ref, dest_ref[j]) if direct else (pair, j)
        for start in range(0, heads, 2):
            group = range(start, min(start + 2, heads))
            update = outer(
                [ready[row, h * NODES : (h + 1) * NODES, :] for h in group],
                [ready[row, (heads + h) * NODES : (heads + h + 1) * NODES, :] for h in group],
                [onpath * jnp.exp(-rates_ref[first + h] * age) for h in group],
            )
            for n, h in enumerate(group):
                at = slice(h * HD, (h + 1) * HD)
                kept = jnp.exp(-rates_ref[first + h] * length) * state[j, at, :]
                fresh[j, at, :] = kept + update[:, n * HD : (n + 1) * HD]
        store(j).start()
        return carry

    lax.fori_loop(0, rows, work, 0, unroll=2)
    for j in range(rows):
        store(j).wait()


def update_states(first, heads, base, dest, rates, path_nodes, states, pairs, partial):
    rows, _, width = states.shape
    earlier = [] if partial is None else [partial]
    direct = pairs.shape[1] == 2 * heads * NODES
    return pl.pallas_call(
        functools.partial(update_kernel, rows, first, heads, base),
        out_shape=jax.ShapeDtypeStruct(states.shape, F32),
        in_specs=[HBM, HBM, HBM, HBM, VMEM if direct else HBM] + [HBM] * len(earlier),
        out_specs=HBM,
        input_output_aliases={5: 0} if earlier else {},
        scratch_shapes=[
            pltpu.VMEM((rows, heads * HD, width), F32),
            pltpu.VMEM((rows, heads * HD, width), F32),
            pltpu.VMEM((1 if direct else rows, 2 * heads * NODES, HD), BF16),
            pltpu.VMEM((rows, NODES, HD), F32),
            pltpu.VMEM((rows, NODES, HD), F32),
            pltpu.VMEM((rows, 8, HD), F32),
            pltpu.SMEM(dest.shape, jnp.int32),
            pltpu.SMEM(rates.shape, F32),
            pltpu.VMEM(path_nodes.shape, jnp.int32),
            pltpu.SemaphoreType.DMA((rows,)),
            pltpu.SemaphoreType.DMA((rows,)),
            pltpu.SemaphoreType.DMA((rows,)),
            pltpu.SemaphoreType.DMA((3,)),
        ],
        compiler_params=pltpu.CompilerParams(vmem_limit_bytes=(49 if direct else 56) << 20),
        cost_estimate=cost(10e6, 5e8),
        name="update_states",
    )(dest, rates, path_nodes, states, pairs, *earlier)


def body(queries, keys, values, states, parents, path_nodes, held, rates, gain):
    me = lax.axis_index("req")
    rows, nodes, width = queries.shape
    heads = width // HD
    flat_states = states.reshape(rows, width, HD)

    def swap(x):
        return lax.all_to_all(x, "req", split_axis=0, concat_axis=0, tiled=True)

    early, late, dest, ids = pack(
        me.reshape(1), held, parents, path_nodes, flat_states, keys, values
    )
    early = swap(early)
    late = swap(gate(late, early))
    attn, square = attend(ids, rates, early, queries, keys, values)
    fresh = update_states(0, EARLY, width, dest, rates, path_nodes, flat_states, early, None)
    head_count = lax.axis_size("head")
    square = square + lax.ppermute(square, "head", [(i, i ^ 1) for i in range(head_count)])
    others = [
        lax.ppermute(square, "head", [(i, (i + step) % head_count) for i in range(head_count)])
        for step in range(2, head_count, 2)
    ]
    square = square + sum(others)
    scaling = lax.rsqrt(square / (HEADS * HD) + EPS)
    mixed = (attn.astype(F32) * scaling[:, :, None] * gain).astype(BF16)
    fresh = update_states(
        EARLY, heads - EARLY, 0, dest, rates, path_nodes, flat_states, late, fresh
    )
    return (mixed, fresh.reshape(rows, heads, HD, HD))


def solution(mesh):
    in_specs = (
        P("req", None, "head"),
        P("req", None, "head"),
        P("req", None, "head"),
        P("req", "head", None, None),
        P("req", None),
        P("req", None),
        P(),
        P("head"),
        P("head"),
    )
    out_specs = (P("req", None, "head"), P("req", "head", None, None))
    return jax.shard_map(body, mesh=mesh, in_specs=in_specs, out_specs=out_specs, check_vma=False)
```

```python
import functools

import jax
import jax.numpy as jnp
from jax import lax
from jax.experimental import pallas as pl
from jax.experimental.pallas import tpu as pltpu
from jax.sharding import PartitionSpec as P

HEADS = 64
HD = 128
NODES = 64
EPS = 1e-06
F32 = jnp.float32
BF16 = jnp.bfloat16
TAIL = 16
FAR = 1e30
EARLY = 4
VMEM_LIMIT = 56 << 20
HBM = pl.BlockSpec(memory_space=pltpu.HBM)
SMEM = pl.BlockSpec(memory_space=pltpu.SMEM)
VMEM = pl.BlockSpec(memory_space=pltpu.VMEM)
PARAMS = pltpu.CompilerParams(vmem_limit_bytes=VMEM_LIMIT)


def dot(a, b, dims=((1,), (0,))):
    return lax.dot_general(a, b, (dims, ((), ())), preferred_element_type=F32)


def cost(bytes_accessed, flops=0, transcendentals=0):
    return pl.CostEstimate(
        flops=int(flops), bytes_accessed=int(bytes_accessed), transcendentals=int(transcendentals)
    )


def path_weights(path, length):
    row = lax.broadcasted_iota(jnp.int32, (NODES, NODES), 0)
    match = (jnp.broadcast_to(path, (NODES, NODES)) == row).astype(F32).astype(BF16)
    place = lax.broadcasted_iota(jnp.int32, (NODES, HD), 0).astype(F32)
    ages = jnp.maximum(length - 1.0 - place, 0.0).astype(BF16)
    both = dot(match, jnp.concatenate([jnp.ones((NODES, HD), BF16), ages], axis=1))
    return both[:, :HD], both[:, HD:]


def diagonal(a, b):
    zero = jnp.zeros(a.shape, a.dtype)
    return jnp.concatenate(
        [jnp.concatenate([a, zero], axis=1), jnp.concatenate([zero, b], axis=1)], axis=0
    )


def parts(v, weight):
    scaled = v.astype(F32) * weight
    high = scaled.astype(BF16)
    return high, (scaled - high.astype(F32)).astype(BF16)


def outer(keys, values, weights):
    split = [parts(v, weight) for v, weight in zip(values, weights)]
    if len(keys) == 1:
        both = dot(keys[0], jnp.concatenate(split[0], axis=1), ((0,), (0,)))
        return both[:, :HD] + both[:, HD:]
    stacked = jnp.concatenate(keys + keys, axis=0)
    spread = [diagonal(split[0][at], split[1][at]) for at in (0, 1)]
    return dot(stacked, jnp.concatenate(spread, axis=0), ((0,), (0,)))


def pack_kernel(
    rows, heads, me_ref, held_hbm, parents_hbm, path_hbm, states_ref, keys_ref, values_ref,
    early_ref, late_ref, dest_hbm, ids_hbm,
    wide, k_all, v_all, early, late, held_ref, parents_ref, path_ref, dest_ref, ids_ref, in_sem, out_sem, small_sem,
):
    height = wide.shape[1]

    def fetch(j):
        return pltpu.make_async_copy(states_ref.at[j], wide.at[j], in_sem.at[3 * j])

    def fetch_pair(j):
        at = ids_ref[dest_ref[j]]
        return (
            pltpu.make_async_copy(keys_ref.at[at], k_all.at[j], in_sem.at[3 * j + 1]),
            pltpu.make_async_copy(values_ref.at[at], v_all.at[j], in_sem.at[3 * j + 2]),
        )

    def store(j):
        return (
            pltpu.make_async_copy(early.at[j], early_ref.at[dest_ref[j]], out_sem.at[2 * j]),
            pltpu.make_async_copy(late.at[j], late_ref.at[dest_ref[j]], out_sem.at[2 * j + 1]),
        )

    held_copy = pltpu.make_async_copy(held_hbm, held_ref, small_sem.at[0])
    tree_copies = (
        pltpu.make_async_copy(parents_hbm, parents_ref, small_sem.at[1]),
        pltpu.make_async_copy(path_hbm, path_ref, small_sem.at[2]),
    )
    index_copies = (
        pltpu.make_async_copy(dest_ref, dest_hbm, small_sem.at[3]),
        pltpu.make_async_copy(ids_ref, ids_hbm, small_sem.at[4]),
    )
    held_copy.start()
    for copy in tree_copies:
        copy.start()
    for j in range(rows):
        fetch(j).start()
    held_copy.wait()
    me = me_ref[0]
    for j in range(rows):
        dest_ref[j] = lax.div(held_ref[me * rows + j], rows)
    for s in range(held_ref.shape[0] // rows):
        found = 0
        for i in range(rows):
            request = held_ref[s * rows + i]
            found = jnp.where(lax.div(request, rows) == me, request - me * rows, found)
        ids_ref[s] = found
    for j in range(rows):
        for copy in fetch_pair(j):
            copy.start()
    for copy in index_copies:
        copy.start()
    for copy in tree_copies:
        copy.wait()

    def work(j, carry):
        fetch(j).wait()
        for copy in fetch_pair(j):
            copy.wait()
        early[j, :height, :] = wide[j].astype(BF16)
        for h in range(heads):
            at = slice(h * HD, (h + 1) * HD)
            base, ref = (height, early) if h < EARLY else (0, late)
            count = EARLY if h < EARLY else heads - EARLY
            h -= 0 if h < EARLY else EARLY
            ref[j, base + h * NODES : base + (h + 1) * NODES, :] = k_all[j, :, at]
            base += count * NODES
            ref[j, base + h * NODES : base + (h + 1) * NODES, :] = v_all[j, :, at]
        both = jnp.concatenate(
            [parents_ref[pl.ds(j, 1), :], path_ref[pl.ds(j, 1), :]], axis=1
        ).astype(F32)
        early[j, height + 2 * EARLY * NODES :, :] = jnp.broadcast_to(both, (TAIL, HD)).astype(BF16)
        for copy in store(j):
            copy.start()
        return carry

    lax.fori_loop(0, rows, work, 0)
    for copy in index_copies:
        copy.wait()
    for j in range(rows):
        for copy in store(j):
            copy.wait()


def pack(me, held, parents, path_nodes, states, keys, values):
    rows, height, width = states.shape
    nodes = keys.shape[1]
    heads = height // HD
    early = (rows, height + 2 * EARLY * nodes + TAIL, width)
    late = (rows, 2 * (heads - EARLY) * nodes, width)
    return pl.pallas_call(
        functools.partial(pack_kernel, rows, heads),
        out_shape=(
            jax.ShapeDtypeStruct(early, BF16),
            jax.ShapeDtypeStruct(late, BF16),
            jax.ShapeDtypeStruct((rows,), jnp.int32),
            jax.ShapeDtypeStruct((held.shape[0] // rows,), jnp.int32),
        ),
        in_specs=[SMEM, HBM, HBM, HBM, HBM, HBM, HBM],
        out_specs=(HBM, HBM, HBM, HBM),
        scratch_shapes=[
            pltpu.VMEM(states.shape, F32),
            pltpu.VMEM(keys.shape, BF16),
            pltpu.VMEM(keys.shape, BF16),
            pltpu.VMEM(early, BF16),
            pltpu.VMEM(late, BF16),
            pltpu.SMEM(held.shape, jnp.int32),
            pltpu.VMEM(parents.shape, jnp.int32),
            pltpu.VMEM(path_nodes.shape, jnp.int32),
            pltpu.SMEM((rows,), jnp.int32),
            pltpu.SMEM((held.shape[0] // rows,), jnp.int32),
            pltpu.SemaphoreType.DMA((3 * rows,)),
            pltpu.SemaphoreType.DMA((2 * rows,)),
            pltpu.SemaphoreType.DMA((5,)),
        ],
        compiler_params=PARAMS,
        cost_estimate=cost(20e6),
        name="pack",
    )(me, held, parents, path_nodes, states, keys, values)


def gate_kernel(value_ref, after_ref, out_ref):
    pass


def gate(value, after):
    return pl.pallas_call(
        gate_kernel,
        out_shape=jax.ShapeDtypeStruct(value.shape, value.dtype),
        in_specs=[HBM, HBM],
        out_specs=HBM,
        input_output_aliases={0: 0},
        compiler_params=PARAMS,
        cost_estimate=cost(1000),
        name="gate",
    )(value, after)


def attend_kernel(
    rows, heads, ids_hbm, rates_hbm, early_ref, q_hbm, k_hbm, v_hbm, attn_ref, square_ref,
    q_all, k_all, v_all, state_all, tails, gaps, depths, weights, ids_ref, rates_ref, sem, tail_sem, small_sem,
):
    tail = early_ref.shape[1] - TAIL
    height = state_all.shape[1]
    tail_copy = pltpu.make_async_copy(early_ref.at[:, pl.ds(tail, TAIL), :], tails, tail_sem)

    def copies(s):
        at = ids_ref[s]
        return (
            pltpu.make_async_copy(q_hbm.at[at], q_all.at[s], sem.at[4 * s]),
            pltpu.make_async_copy(k_hbm.at[at], k_all.at[s], sem.at[4 * s + 1]),
            pltpu.make_async_copy(v_hbm.at[at], v_all.at[s], sem.at[4 * s + 2]),
            pltpu.make_async_copy(
                early_ref.at[s, pl.ds(0, height), :], state_all.at[s], sem.at[4 * s + 3]
            ),
        )

    ids_copy = pltpu.make_async_copy(ids_hbm, ids_ref, small_sem.at[0])
    rates_copy = pltpu.make_async_copy(rates_hbm, rates_ref, small_sem.at[1])
    ids_copy.start()
    rates_copy.start()
    tail_copy.start()
    ids_copy.wait()
    for s in range(rows):
        for copy in copies(s):
            copy.start()
    rates_copy.wait()
    tail_copy.wait()

    row = lax.broadcasted_iota(jnp.int32, (NODES, NODES), 0)
    col = lax.broadcasted_iota(jnp.int32, (NODES, NODES), 1)
    row_wide = row.astype(F32)
    eye = (row == col).astype(F32)
    batch = rows

    def grow(group, carry):
        steps, reaches = [], []
        for b in range(batch):
            parents = tails[group * batch + b].astype(F32)[0:1, :NODES]
            step = (jnp.broadcast_to(parents, (NODES, NODES)) == row_wide).astype(F32)
            steps.append(step.astype(BF16))
            reaches.append(eye + step)
        hops = 2
        while hops < NODES:
            steps = [dot(x, x).astype(BF16) for x in steps]
            reaches = [r + dot(x, r.astype(BF16)) for x, r in zip(steps, reaches)]
            hops *= 2
        for b in range(batch):
            s = group * batch + b
            reach = reaches[b].T
            depth_row = jnp.sum(reaches[b], axis=0, keepdims=True)
            depth = jnp.sum(reach, axis=1, keepdims=True)
            gap = jnp.where(reach > 0.5, depth - depth_row, FAR)
            gaps[s] = jnp.concatenate([gap, gap], axis=1)
            depths[s] = jnp.broadcast_to(depth, (NODES, HD))
        return carry

    lax.fori_loop(0, rows // batch, grow, 0)

    lane = lax.broadcasted_iota(jnp.int32, (1, HD), 1)

    def score(s, carry):
        for copy in copies(s):
            copy.wait()
        gap = gaps[s]
        for pair in range(heads // 2):
            a = slice(2 * pair * HD, (2 * pair + 1) * HD)
            b = slice((2 * pair + 1) * HD, (2 * pair + 2) * HD)
            q = q_all[s, :, 2 * pair * HD : (2 * pair + 2) * HD]
            scores = dot(q, diagonal(k_all[s, :, a], k_all[s, :, b]), ((1,), (1,)))
            rate = jnp.where(lane < NODES, rates_ref[2 * pair], rates_ref[2 * pair + 1])
            weights[s, pair] = (scores * jnp.exp(-rate * gap)).astype(BF16)
        return carry

    def finish(s, carry):
        depth = depths[s]
        at_row = ids_ref[s]
        total = jnp.zeros((NODES, HD), F32)
        for pair in range(heads // 2):
            a = slice(2 * pair * HD, (2 * pair + 1) * HD)
            b = slice((2 * pair + 1) * HD, (2 * pair + 2) * HD)
            q = q_all[s, :, 2 * pair * HD : (2 * pair + 2) * HD]
            local = dot(weights[s, pair], diagonal(v_all[s, :, a], v_all[s, :, b]))
            prior = dot(q, diagonal(state_all[s, a, :], state_all[s, b, :]))
            for h, at, cut in ((2 * pair, a, slice(0, HD)), (2 * pair + 1, b, slice(HD, 2 * HD))):
                decay = jnp.exp(-rates_ref[h] * depth)
                attn = (local[:, cut] + prior[:, cut] * decay).astype(BF16)
                attn_ref[at_row, :, at] = attn
                wide = attn.astype(F32)
                total = total + wide * wide
        square_ref[pl.ds(at_row, 1), :] = jnp.sum(total.T, axis=0, keepdims=True)
        return carry

    lax.fori_loop(0, rows, score, 0, unroll=2)
    lax.fori_loop(0, rows, finish, 0, unroll=2)


def attend(ids, rates, early, queries, keys, values):
    rows, nodes, width = queries.shape
    return pl.pallas_call(
        functools.partial(attend_kernel, rows, width // HD),
        out_shape=(
            jax.ShapeDtypeStruct((rows, nodes, width), BF16),
            jax.ShapeDtypeStruct((rows, nodes), F32),
        ),
        in_specs=[HBM, HBM, HBM, HBM, HBM, HBM],
        out_specs=(VMEM, VMEM),
        scratch_shapes=[
            pltpu.VMEM((rows, nodes, width), BF16),
            pltpu.VMEM((rows, nodes, width), BF16),
            pltpu.VMEM((rows, nodes, width), BF16),
            pltpu.VMEM((rows, width, HD), BF16),
            pltpu.VMEM((rows, TAIL, HD), BF16),
            pltpu.VMEM((rows, nodes, 2 * nodes), F32),
            pltpu.VMEM((rows, nodes, HD), F32),
            pltpu.VMEM((rows, width // HD // 2, nodes, 2 * nodes), BF16),
            pltpu.SMEM(ids.shape, jnp.int32),
            pltpu.SMEM(rates.shape, F32),
            pltpu.SemaphoreType.DMA((4 * rows,)),
            pltpu.SemaphoreType.DMA,
            pltpu.SemaphoreType.DMA((2,)),
        ],
        compiler_params=PARAMS,
        cost_estimate=cost(50e6, 1e9),
        name="attend",
    )(ids, rates, early, queries, keys, values)


def update_kernel(
    rows, first, heads, base, dest_hbm, rates_hbm, path_hbm, states_ref, pairs_ref, *refs
):
    out_ref, state, fresh, pair, onpaths, ages, lengths = refs[-14:-7]
    dest_ref, rates_ref, path_ref, in_sem, pair_sem, out_sem, small_sem = refs[-7:]
    direct = pair.shape[0] == 1
    part = pl.ds(first * HD, heads * HD)

    def fetch(j):
        copies = [pltpu.make_async_copy(states_ref.at[j, part, :], state.at[j], in_sem.at[j])]
        if not direct:
            source = pairs_ref.at[dest_ref[j], pl.ds(base, 2 * heads * NODES), :]
            copies.append(pltpu.make_async_copy(source, pair.at[j], pair_sem.at[j]))
        return copies

    def store(j):
        return pltpu.make_async_copy(fresh.at[j], out_ref.at[j, part, :], out_sem.at[j])

    small = [
        pltpu.make_async_copy(source, target, small_sem.at[n])
        for n, (source, target) in enumerate(
            ((dest_hbm, dest_ref), (path_hbm, path_ref), (rates_hbm, rates_ref))
        )
    ]
    for copy in small:
        copy.start()
    ahead = rows if direct else rows // 2
    if not direct:
        small[0].wait()
    for j in range(ahead):
        for copy in fetch(j):
            copy.start()
    for copy in small[0 if direct else 1 :]:
        copy.wait()

    counts = jnp.sum((path_ref[...] >= 0).astype(F32), axis=1, keepdims=True)
    counts = jnp.broadcast_to(counts, (rows, HD))
    for j in range(rows):
        length = counts[j : j + 1, :]
        onpaths[j], ages[j] = path_weights(path_ref[j : j + 1, :], length)
        lengths[j] = jnp.broadcast_to(length, (8, HD))
    for j in range(ahead, rows):
        for copy in fetch(j):
            copy.start()

    def work(j, carry):
        onpath, age, length = onpaths[j], ages[j], lengths[j, 0:1, :]
        for copy in fetch(j):
            copy.wait()
        ready, row = (pairs_ref, dest_ref[j]) if direct else (pair, j)
        for start in range(0, heads, 2):
            group = range(start, min(start + 2, heads))
            update = outer(
                [ready[row, h * NODES : (h + 1) * NODES, :] for h in group],
                [ready[row, (heads + h) * NODES : (heads + h + 1) * NODES, :] for h in group],
                [onpath * jnp.exp(-rates_ref[first + h] * age) for h in group],
            )
            for n, h in enumerate(group):
                at = slice(h * HD, (h + 1) * HD)
                kept = jnp.exp(-rates_ref[first + h] * length) * state[j, at, :]
                fresh[j, at, :] = kept + update[:, n * HD : (n + 1) * HD]
        store(j).start()
        return carry

    lax.fori_loop(0, rows, work, 0, unroll=2)
    for j in range(rows):
        store(j).wait()


def update_states(first, heads, base, dest, rates, path_nodes, states, pairs, partial):
    rows, _, width = states.shape
    earlier = [] if partial is None else [partial]
    direct = pairs.shape[1] == 2 * heads * NODES
    return pl.pallas_call(
        functools.partial(update_kernel, rows, first, heads, base),
        out_shape=jax.ShapeDtypeStruct(states.shape, F32),
        in_specs=[HBM, HBM, HBM, HBM, VMEM if direct else HBM] + [HBM] * len(earlier),
        out_specs=HBM,
        input_output_aliases={5: 0} if earlier else {},
        scratch_shapes=[
            pltpu.VMEM((rows, heads * HD, width), F32),
            pltpu.VMEM((rows, heads * HD, width), F32),
            pltpu.VMEM((1 if direct else rows, 2 * heads * NODES, HD), BF16),
            pltpu.VMEM((rows, NODES, HD), F32),
            pltpu.VMEM((rows, NODES, HD), F32),
            pltpu.VMEM((rows, 8, HD), F32),
            pltpu.SMEM(dest.shape, jnp.int32),
            pltpu.SMEM(rates.shape, F32),
            pltpu.VMEM(path_nodes.shape, jnp.int32),
            pltpu.SemaphoreType.DMA((rows,)),
            pltpu.SemaphoreType.DMA((rows,)),
            pltpu.SemaphoreType.DMA((rows,)),
            pltpu.SemaphoreType.DMA((3,)),
        ],
        compiler_params=pltpu.CompilerParams(vmem_limit_bytes=(49 if direct else 56) << 20),
        cost_estimate=cost(10e6, 5e8),
        name="update_states",
    )(dest, rates, path_nodes, states, pairs, *earlier)


def body(queries, keys, values, states, parents, path_nodes, held, rates, gain):
    me = lax.axis_index("req")
    rows, nodes, width = queries.shape
    heads = width // HD
    flat_states = states.reshape(rows, width, HD)

    def swap(x):
        return lax.all_to_all(x, "req", split_axis=0, concat_axis=0, tiled=True)

    early, late, dest, ids = pack(
        me.reshape(1), held, parents, path_nodes, flat_states, keys, values
    )
    early = swap(early)
    late = swap(gate(late, early))
    attn, square = attend(ids, rates, early, queries, keys, values)
    fresh = update_states(0, EARLY, width, dest, rates, path_nodes, flat_states, early, None)
    head_count = lax.axis_size("head")
    square = square + lax.ppermute(square, "head", [(i, i ^ 1) for i in range(head_count)])
    others = [
        lax.ppermute(square, "head", [(i, (i + step) % head_count) for i in range(head_count)])
        for step in range(2, head_count, 2)
    ]
    square = square + sum(others)
    scaling = lax.rsqrt(square / (HEADS * HD) + EPS)
    mixed = (attn.astype(F32) * scaling[:, :, None] * gain).astype(BF16)
    fresh = update_states(
        EARLY, heads - EARLY, 0, dest, rates, path_nodes, flat_states, late, fresh
    )
    return (mixed, fresh.reshape(rows, heads, HD, HD))


def solution(mesh):
    in_specs = (
        P("req", None, "head"),
        P("req", None, "head"),
        P("req", None, "head"),
        P("req", "head", None, None),
        P("req", None),
        P("req", None),
        P(),
        P("head"),
        P("head"),
    )
    out_specs = (P("req", None, "head"), P("req", "head", None, None))
    return jax.shard_map(body, mesh=mesh, in_specs=in_specs, out_specs=out_specs, check_vma=False)
```
